32 devices in a mesh: fsdp: 16 (over z, y, core), dp: 2 (over x).
Axes of the slice: x: 2, y: 2, z: 4, core: 2. Of those that a mesh axis runs over, the one named last changes fastest.
Arguments:
- acts: bfloat16 [2048, 4096], P(('dp', 'fsdp')), may hold values from -6 to 6
- out_grad: bfloat16 [2048, 4096], P(('dp', 'fsdp')), may hold values from -6 to 6
- gate_weight: bfloat16 [14336, 4096], P('fsdp'), may hold values from -0.09375 to 0.09375
- up_weight: bfloat16 [14336, 4096], P('fsdp'), may hold values from -0.09375 to 0.09375
- proj_in: bfloat16 [14336, 64], P('fsdp'), may hold values from -0.046875 to 0.046875
- proj_out: bfloat16 [4096, 64], replicated, may hold values from -0.09375 to 0.09375
Outputs:
- features: float32 [4, 4096], P('dp', 'fsdp')
- gram: float32 [4096, 4096], P('fsdp', 'dp')
The draws below stay inside these ranges and needn't reach their ends.
All inputs are finite; a program needn't handle non-finite values.
Results may differ from the reference program's by a relative error of at most 0.0038.
Values may be sent and summed in bfloat16 or wider, within the bound.
A program may use at most 128 MiB of HBM per device.

```python
import jax
import jax.numpy as jnp
from jax import lax

D = 4096
FF = 14336
KP = 64
KQ = 64
LEN = 512
TOKENS = 2048


def level_of(key, dims, shards, smallest, largest):
    gain = 1.0
    for axis_at, blocks in shards:
        steps = jax.random.uniform(jax.random.fold_in(jax.random.fold_in(key, 6), axis_at), (blocks,), jnp.float32, smallest / len(shards), largest / len(shards))
        gain = gain * jnp.repeat(jnp.exp(steps), dims[axis_at] // blocks).reshape((-1,) + (1,) * (len(dims) - 1 - axis_at))
    return gain


def centred(stream_key, shape, width, limit, shards=(), held_as=jnp.bfloat16):
    values = width * jax.random.normal(stream_key, shape, jnp.float32)
    if shards:
        values = values * level_of(stream_key, shape, shards, -0.22, 0.18)
    return jnp.clip(values, -limit, limit).astype(held_as)


def setup_inputs(seed: int = 0) -> dict:
    streams_of = jax.random.split(jax.random.key(seed), 7)
    acts = centred(streams_of[0], (TOKENS, D), 1.0, 6.0, ((0, 32),))
    out_grad = centred(streams_of[1], (TOKENS, D), 1.0, 6.0, ((0, 32),))
    gate_weight = centred(streams_of[2], (FF, D), D ** -0.5, 0.09375, ((0, 16),))
    up_weight = centred(streams_of[3], (FF, D), D ** -0.5, 0.09375, ((0, 16),))
    proj_in = centred(streams_of[4], (FF, KP), FF ** -0.5, 0.046875, ((0, 16),))
    proj_out = centred(streams_of[5], (D, KQ), D ** -0.5, 0.09375)
    return {"acts": acts, "out_grad": out_grad, "gate_weight": gate_weight, "up_weight": up_weight, "proj_in": proj_in, "proj_out": proj_out}


def reference(acts, out_grad, gate_weight, up_weight, proj_in, proj_out):
    examples = acts.shape[0] // LEN
    inputs = acts.reshape(examples, LEN, D)
    grads = out_grad.reshape(examples, LEN, D)

    def project(pair):
        tok_in, tok_grad = pair
        gate = jnp.dot(tok_in, gate_weight.T, preferred_element_type=jnp.float32)
        upper = jnp.dot(tok_in, up_weight.T, preferred_element_type=jnp.float32)
        hidden = (jax.nn.silu(gate) * upper).astype(jnp.bfloat16)
        return (jnp.dot(hidden, proj_in, preferred_element_type=jnp.float32), jnp.dot(tok_grad, proj_out, preferred_element_type=jnp.float32))
    left, right = lax.map(project, (inputs, grads))
    raw = jnp.einsum('elp,elq->epq', left, right, precision=lax.Precision.HIGHEST).reshape(examples, KP * KQ)
    features = raw / jnp.sqrt(lax.optimization_barrier(jnp.sum(raw * raw, axis=1, keepdims=True)) + 1e-06)

    def accumulate(total, pair):
        u_rows, v_rows = pair
        zeta = (u_rows[:, :, None] * v_rows[:, None, :]).reshape(LEN, KP * KQ)
        return (total + jnp.dot(zeta.T, zeta, precision=lax.Precision.HIGHEST, preferred_element_type=jnp.float32), None)
    gram, _ = lax.scan(accumulate, jnp.zeros((KP * KQ, KP * KQ), jnp.float32), (left, right))
    gram = gram / jnp.float32(examples * LEN)
    return (features, gram)
```

```python
import functools

import jax
import jax.numpy as jnp
from jax import lax
from jax.experimental import pallas as pl
from jax.experimental.pallas import tpu as pltpu
from jax.sharding import PartitionSpec as P

LEN = 512


def outer_rows(u_part, v_rows):
    return (u_part[:, :, None] * v_rows[:, None, :]).reshape(
        u_part.shape[0], u_part.shape[1] * v_rows.shape[1]
    )


def moment_rows(u_part, u_cols, v_rows):
    a_rows = outer_rows(u_part, v_rows)
    z_cols = outer_rows(u_cols, v_rows)
    return lax.dot_general(
        a_rows,
        z_cols,
        (((0,), (0,)), ((), ())),
        precision=lax.Precision.HIGHEST,
        preferred_element_type=jnp.float32,
    )


def local(acts, out_grad, gate_weight, up_weight, proj_in, proj_out):
    n_fsdp = lax.axis_size("fsdp")
    n_dp = lax.axis_size("dp")
    contract = (((1,), (1,)), ((), ()))
    piece = lax.all_gather(acts, "fsdp", axis=0, tiled=True)
    gate = lax.dot_general(piece, gate_weight, contract, preferred_element_type=jnp.float32)
    upper = lax.dot_general(piece, up_weight, contract, preferred_element_type=jnp.float32)
    hidden = (jax.nn.silu(gate) * upper).astype(jnp.bfloat16)
    part_in = jnp.dot(hidden, proj_in, preferred_element_type=jnp.float32)
    left = lax.psum(part_in, "fsdp")
    part_out = jnp.dot(out_grad, proj_out, preferred_element_type=jnp.float32)
    right = lax.all_gather(part_out, "fsdp", axis=0, tiled=True)
    rows = left.shape[0]
    total_tokens = rows * n_dp
    kp_size = left.shape[1]
    kq_size = right.shape[1]
    row_width = kp_size // n_fsdp
    first = lax.axis_index("fsdp") * row_width
    mine = lax.dynamic_slice_in_dim(left, first, row_width, 1)
    examples = rows // LEN
    left_ex = left.reshape(examples, LEN, kp_size)
    right_ex = right.reshape(examples, LEN, kq_size)
    mine_ex = mine.reshape(examples, LEN, row_width)
    raw = jnp.einsum("elw,elq->ewq", mine_ex, right_ex, precision=lax.Precision.HIGHEST).reshape(
        examples, row_width * kq_size
    )
    squared = lax.psum(jnp.sum(raw * raw, axis=1), "fsdp")
    features = raw / jnp.sqrt(squared + 1e-06)[:, None]

    def add_example(index, total):
        u_rows = lax.dynamic_index_in_dim(left_ex, index, 0, keepdims=False)
        v_rows = lax.dynamic_index_in_dim(right_ex, index, 0, keepdims=False)
        u_part = lax.dynamic_index_in_dim(mine_ex, index, 0, keepdims=False)
        return total + moment_rows(u_part, u_rows, v_rows)

    start_total = jnp.zeros((row_width * kq_size, kp_size * kq_size), jnp.float32)
    partial_value = lax.fori_loop(0, examples, add_example, start_total)
    gram = lax.psum_scatter(
        partial_value / jnp.float32(total_tokens), "dp", scatter_dimension=1, tiled=True
    )
    return (features, gram)


MESH = pl.DeviceIdType.MESH
NT = (((1,), (1,)), ((), ()))
NN = (((1,), (0,)), ((), ()))
F32 = jnp.float32
BF16 = jnp.bfloat16
PLANE = 4


def fused_kernel(n_f, n_dp, acts, out_grad, gate_w, up_w, proj_in, proj_out, feat, gram,
                 xbuf, wbuf, pin, og, part, lrecv, rbuf, lbuf, ut, vt, raw_s,
                 own_sem, w_sem, zr_sem, yr_sem, cr_sem, zu_s, zd_s, ys_s, cs_s,
                 part_s, part_r, r_s, r_r, l_s, l_r):
    n_z = n_f // PLANE
    n_all = n_f * n_dp
    rows = acts.shape[0]
    units = gate_w.shape[0]
    n_chunk = units // 128
    prow = rows * PLANE
    kp = proj_in.shape[0]
    kq = proj_out.shape[0]
    d = lax.axis_index("dp")
    f = lax.axis_index("fsdp")
    g = d * n_f + f
    z = f // PLANE
    y = (f // 2) % 2
    c = f % 2
    h = g // 2
    n_chip = n_all // 2

    def at(fi):
        return {"dp": d, "fsdp": fi}

    def device(gi):
        return {"dp": gi // n_f, "fsdp": gi % n_f}

    own = pltpu.make_async_copy(acts, xbuf.at[f], own_sem.at[0])
    own.start()
    ogc = pltpu.make_async_copy(out_grad, og, own_sem.at[1])
    ogc.start()
    weights = []
    for k in range(n_chunk):
        for s, w in enumerate((gate_w, up_w)):
            cp = pltpu.make_async_copy(
                w.at[pl.ds(128 * k, 128)], wbuf.at[k, pl.ds(128 * s, 128)], w_sem.at[2 * k + s]
            )
            cp.start()
            weights.append(cp)

    barrier = pltpu.get_barrier_semaphore()

    def greet(o, carry):
        pl.semaphore_signal(barrier, inc=1, device_id=device((g + o) % n_all), device_id_type=MESH)
        return carry

    lax.fori_loop(1, n_all, greet, 0)
    pl.semaphore_wait(barrier, n_all - 1)

    def push(block, target, send, recv):
        return pltpu.make_async_remote_copy(
            src_ref=xbuf.at[block], dst_ref=xbuf.at[block], send_sem=send, recv_sem=recv,
            device_id=at(target), device_id_type=MESH,
        )

    def z_up(p):
        return push(p * PLANE + y * 2 + c, f + PLANE, zu_s.at[p], zr_sem.at[p])

    def z_down(p):
        return push(p * PLANE + y * 2 + c, f - PLANE, zd_s.at[p], zr_sem.at[p])

    def y_send(p):
        return push(p * PLANE + y * 2 + c, z * PLANE + (1 - y) * 2 + c, ys_s.at[p], yr_sem.at[p])

    def c_send(p, yy):
        return push(p * PLANE + yy * 2 + c, z * PLANE + y * 2 + 1 - c, cs_s.at[2 * p + yy], cr_sem.at[2 * p + yy])

    def when(cond, fn):
        if cond is None:
            fn()
        else:
            pl.when(cond)(fn)

    def planes(r):
        if r == 0:
            return [(z, None, 0)]
        return [(z - r, z - r >= 0, 1), (z + r, z + r < n_z, -1)]

    def spread(r):
        for p, ok, way in planes(r):
            def go(p=p, way=way):
                if way != 0:
                    z_up(p).wait_recv()
                if way >= 0:
                    pl.when(z < n_z - 1)(lambda: z_up(p).start())
                if way <= 0:
                    pl.when(z > 0)(lambda: z_down(p).start())
                y_send(p).start()
                c_send(p, y).start()
            when(ok, go)

    def part_copy(p, q):
        return pltpu.make_async_remote_copy(
            src_ref=part.at[p, pl.ds(16 * q, 16)], dst_ref=lrecv.at[f],
            send_sem=part_s.at[p * PLANE + q], recv_sem=part_r.at[f],
            device_id=at(p * PLANE + q), device_id_type=MESH,
        )

    def work(r):
        for p, ok, _ in planes(r):
            def relay(p=p):
                y_send(p).wait_recv()
                c_send(p, 1 - y).start()
            when(ok, relay)
        for p, ok, _ in planes(r):
            def go(p=p):
                c_send(p, 0).wait_recv()
                c_send(p, 1).wait_recv()

                def chunk(k, total):
                    x = xbuf[pl.ds(p * PLANE, PLANE)].reshape(prow, acts.shape[1])
                    both = lax.dot_general(wbuf[k], x, NT, preferred_element_type=F32)
                    gate = both[:128]
                    hidden = (gate / (1.0 + jnp.exp(-gate)) * both[128:]).astype(BF16)
                    return total + lax.dot_general(pin[k], hidden, NN, preferred_element_type=F32)

                total = lax.fori_loop(0, n_chunk, chunk, jnp.zeros((kp, prow), F32))
                part[p] = total
                for q in range(PLANE):
                    mine = p * PLANE + q == f
                    pl.when(jnp.logical_not(mine))(lambda q=q: part_copy(p, q).start())

                    def keep(q=q):
                        lrecv[f] = part[p, pl.ds(16 * q, 16)]
                    pl.when(mine)(keep)
            when(ok, go)

    own.wait()
    spread(0)

    ogc.wait()
    for k in range(n_chunk):
        pin[k] = proj_in[:, pl.ds(128 * k, 128)]
    right = lax.dot_general(og[...], proj_out[...], NT, preferred_element_type=F32)
    rbuf[c, h] = jnp.concatenate([right[:rows // 2], right[rows // 2:]], axis=1)

    def share(buf, send, recv, o):
        return pltpu.make_async_remote_copy(
            src_ref=buf.at[c, h], dst_ref=buf.at[c, h], send_sem=send.at[o], recv_sem=recv.at[o],
            device_id=device(((h + o) % n_chip) * 2 + c), device_id_type=MESH,
        )

    def swap(buf, send, recv):
        return pltpu.make_async_remote_copy(
            src_ref=buf.at[c], dst_ref=buf.at[c], send_sem=send.at[0], recv_sem=recv.at[0],
            device_id=at(f + 1 - 2 * c), device_id_type=MESH,
        )

    def each(fn):
        def body(o, carry):
            fn(o)
            return carry
        lax.fori_loop(1, n_chip, body, 0)

    each(lambda o: share(rbuf, r_s, r_r, o).start())
    for cp in weights:
        cp.wait()

    for r in range(1, n_z):
        spread(r)
        work(r - 1)
        if r == 1:
            each(lambda o: share(rbuf, r_s, r_r, o).wait())
            swap(rbuf, r_s, r_r).start()

    swap(rbuf, r_s, r_r).wait()
    lane = lax.broadcasted_iota(jnp.int32, (kq, 2 * rows), 1)
    low = lane // (rows // 2) % 2 == 0
    for b in range(n_chip):
        one, two = rbuf[0, b], rbuf[1, b]
        tall = jnp.concatenate([one, one, two, two], axis=0).T
        vt[:, pl.ds(2 * rows * b, 2 * rows)] = jnp.where(low, tall[:kq], tall[kq:])
    work(n_z - 1)

    def wait_part(s, carry):
        def go():
            pltpu.make_async_remote_copy(
                src_ref=lrecv.at[s], dst_ref=lrecv.at[s], send_sem=part_s.at[s], recv_sem=part_r.at[s],
                device_id=at(f), device_id_type=MESH,
            ).wait_recv()
        pl.when(s != f)(go)
        return carry

    lax.fori_loop(0, n_f, wait_part, 0)
    total = lrecv[0]
    for s in range(1, n_f):
        total = total + lrecv[s]
    lbuf[c, h] = total
    each(lambda o: share(lbuf, l_s, l_r, o).start())
    each(lambda o: share(lbuf, l_s, l_r, o).wait())
    swap(lbuf, l_s, l_r).start()
    swap(lbuf, l_s, l_r).wait()

    for b in range(n_all):
        q = b % PLANE
        tok = (b // n_f) * n_z + (b % n_f) // PLANE
        ut[pl.ds(16 * q, 16), pl.ds(prow * tok, prow)] = lbuf[b % 2, b // 2]

    width = kp // n_f
    cols = kp // n_dp
    tokens = ut.shape[1]
    group = tokens // n_dp

    def z_rows(first, count):
        v = vt[...]
        return jnp.concatenate([(ut[pl.ds(first + i, 1), :] * v).astype(BF16) for i in range(count)], axis=0)

    a_rows = z_rows(f * width, width)
    for k in range(cols // 4):
        z_cols = z_rows(d * cols + 4 * k, 4)
        block = lax.dot_general(a_rows, z_cols, NT, preferred_element_type=F32)
        gram[:, pl.ds(4 * kq * k, 4 * kq)] = block * (1.0 / tokens)

    for e in range(group // LEN):
        span = pl.ds(pl.multiple_of(d * group + e * LEN, LEN), LEN)
        raw = lax.dot_general(ut[:, span], vt[:, span], NT, precision=lax.Precision.HIGHEST, preferred_element_type=F32)
        norm = jnp.sqrt(jnp.sum(raw * raw, keepdims=True) + 1e-06)
        raw_s[...] = raw / norm
        for i in range(width):
            feat[e, pl.ds(i, 1), :] = raw_s[pl.ds(f * width + i, 1), :]

    for r in range(n_z):
        for p, ok, way in planes(r):
            def fin(p=p, way=way):
                if way >= 0:
                    pl.when(z < n_z - 1)(lambda: z_up(p).wait_send())
                if way <= 0:
                    pl.when(z > 0)(lambda: z_down(p).wait_send())
                y_send(p).wait_send()
                c_send(p, 0).wait_send()
                c_send(p, 1).wait_send()
                for q in range(PLANE):
                    pl.when(p * PLANE + q != f)(lambda q=q: part_copy(p, q).wait_send())
            when(ok, fin)


def fused(n_f, n_dp, acts, out_grad, gate_weight, up_weight, proj_in, proj_out):
    rows, depth = acts.shape
    units = gate_weight.shape[0]
    kp, kq = proj_in.shape[1], proj_out.shape[1]
    n_all = n_f * n_dp
    tokens = rows * n_all
    n_chunk = units // 128
    n_z = n_f // PLANE
    width = kp // n_f
    examples = rows * n_f // LEN
    dma = pltpu.SemaphoreType.DMA
    hbm = pl.BlockSpec(memory_space=pl.ANY)
    vmem = pl.BlockSpec(memory_space=pltpu.VMEM)
    features, gram = pl.pallas_call(
        functools.partial(fused_kernel, n_f, n_dp),
        out_shape=(
            jax.ShapeDtypeStruct((examples, width, kq), F32),
            jax.ShapeDtypeStruct((width * kq, kp * kq // n_dp), F32),
        ),
        in_specs=[hbm, hbm, hbm, hbm, vmem, vmem],
        out_specs=(vmem, vmem),
        scratch_shapes=[
            pltpu.VMEM((n_f, rows, depth), BF16),
            pltpu.VMEM((n_chunk, 256, depth), BF16),
            pltpu.VMEM((n_chunk, kp, 128), BF16),
            pltpu.VMEM((rows, depth), BF16),
            pltpu.VMEM((n_z, kp, rows * PLANE), F32),
            pltpu.VMEM((n_f, 16, rows * PLANE), F32),
            pltpu.VMEM((2, n_all // 2, rows // 2, 2 * kq), F32),
            pltpu.VMEM((2, n_all // 2, 16, rows * PLANE), F32),
            pltpu.VMEM((kp, tokens), F32),
            pltpu.VMEM((kq, tokens), F32),
            pltpu.VMEM((kp, kq), F32),
            dma((2,)), dma((2 * n_chunk,)), dma((n_z,)), dma((n_z,)), dma((2 * n_z,)),
            dma((n_z,)), dma((n_z,)), dma((n_z,)), dma((2 * n_z,)),
            dma((n_f,)), dma((n_f,)), dma((n_all // 2,)), dma((n_all // 2,)), dma((n_all // 2,)), dma((n_all // 2,)),
        ],
        compiler_params=pltpu.CompilerParams(
            collective_id=0, has_side_effects=True, vmem_limit_bytes=56 * 1024 * 1024
        ),
    )(acts, out_grad, gate_weight, up_weight, proj_in.T, proj_out.T)
    return features.reshape(examples, width * kq), gram


def solution(mesh):
    n_f, n_dp = mesh.shape["fsdp"], mesh.shape["dp"]

    def run(acts, out_grad, gate_weight, up_weight, proj_in, proj_out):
        rows, units = acts.shape[0], gate_weight.shape[0]
        fits = (
            n_f % PLANE == 0
            and (PLANE * rows) % 128 == 0
            and units % 128 == 0
            and proj_out.shape[1] == 64
            and (2 * rows) % 128 == 0
            and proj_in.shape[1] == 16 * PLANE
            and proj_in.shape[1] % n_f == 0
            and proj_in.shape[1] % (4 * n_dp) == 0
            and (rows * n_f) % LEN == 0
        )
        if fits:
            return fused(n_f, n_dp, acts, out_grad, gate_weight, up_weight, proj_in, proj_out)
        return local(acts, out_grad, gate_weight, up_weight, proj_in, proj_out)

    in_specs = (
        P(("dp", "fsdp"), None),
        P(("dp", "fsdp"), None),
        P("fsdp", None),
        P("fsdp", None),
        P("fsdp", None),
        P(),
    )
    out_specs = (P("dp", "fsdp"), P("fsdp", "dp"))
    return jax.shard_map(run, mesh=mesh, in_specs=in_specs, out_specs=out_specs, check_vma=False)
```

```python
import functools

import jax
import jax.numpy as jnp
from jax import lax
from jax.experimental import pallas as pl
from jax.experimental.pallas import tpu as pltpu
from jax.sharding import PartitionSpec as P

LEN = 512


def outer_rows(u_part, v_rows):
    return (u_part[:, :, None] * v_rows[:, None, :]).reshape(
        u_part.shape[0], u_part.shape[1] * v_rows.shape[1]
    )


def moment_rows(u_part, u_cols, v_rows):
    a_rows = outer_rows(u_part, v_rows)
    z_cols = outer_rows(u_cols, v_rows)
    return lax.dot_general(
        a_rows,
        z_cols,
        (((0,), (0,)), ((), ())),
        precision=lax.Precision.HIGHEST,
        preferred_element_type=jnp.float32,
    )


def local(acts, out_grad, gate_weight, up_weight, proj_in, proj_out):
    n_fsdp = lax.axis_size("fsdp")
    n_dp = lax.axis_size("dp")
    contract = (((1,), (1,)), ((), ()))
    piece = lax.all_gather(acts, "fsdp", axis=0, tiled=True)
    gate = lax.dot_general(piece, gate_weight, contract, preferred_element_type=jnp.float32)
    upper = lax.dot_general(piece, up_weight, contract, preferred_element_type=jnp.float32)
    hidden = (jax.nn.silu(gate) * upper).astype(jnp.bfloat16)
    part_in = jnp.dot(hidden, proj_in, preferred_element_type=jnp.float32)
    left = lax.psum(part_in, "fsdp")
    part_out = jnp.dot(out_grad, proj_out, preferred_element_type=jnp.float32)
    right = lax.all_gather(part_out, "fsdp", axis=0, tiled=True)
    rows = left.shape[0]
    total_tokens = rows * n_dp
    kp_size = left.shape[1]
    kq_size = right.shape[1]
    row_width = kp_size // n_fsdp
    first = lax.axis_index("fsdp") * row_width
    mine = lax.dynamic_slice_in_dim(left, first, row_width, 1)
    examples = rows // LEN
    left_ex = left.reshape(examples, LEN, kp_size)
    right_ex = right.reshape(examples, LEN, kq_size)
    mine_ex = mine.reshape(examples, LEN, row_width)
    raw = jnp.einsum("elw,elq->ewq", mine_ex, right_ex, precision=lax.Precision.HIGHEST).reshape(
        examples, row_width * kq_size
    )
    squared = lax.psum(jnp.sum(raw * raw, axis=1), "fsdp")
    features = raw / jnp.sqrt(squared + 1e-06)[:, None]

    def add_example(index, total):
        u_rows = lax.dynamic_index_in_dim(left_ex, index, 0, keepdims=False)
        v_rows = lax.dynamic_index_in_dim(right_ex, index, 0, keepdims=False)
        u_part = lax.dynamic_index_in_dim(mine_ex, index, 0, keepdims=False)
        return total + moment_rows(u_part, u_rows, v_rows)

    start_total = jnp.zeros((row_width * kq_size, kp_size * kq_size), jnp.float32)
    partial_value = lax.fori_loop(0, examples, add_example, start_total)
    gram = lax.psum_scatter(
        partial_value / jnp.float32(total_tokens), "dp", scatter_dimension=1, tiled=True
    )
    return (features, gram)


MESH = pl.DeviceIdType.MESH
NT = (((1,), (1,)), ((), ()))
NN = (((1,), (0,)), ((), ()))
F32 = jnp.float32
BF16 = jnp.bfloat16
PLANE = 4


def fused_kernel(n_f, n_dp, acts, out_grad, gate_w, up_w, proj_in, proj_out, ut, vt,
                 xbuf, wbuf, pin, og, part, lrecv, rbuf, lbuf,
                 own_sem, w_sem, zr_sem, yr_sem, cr_sem, zu_s, zd_s, ys_s, cs_s, w_s, w_r,
                 part_s, part_r, r_s, r_r, l_s, l_r):
    n_z = n_f // PLANE
    n_all = n_f * n_dp
    rows = acts.shape[0]
    units = gate_w.shape[0]
    n_chunk = units // 128
    prow = rows * PLANE
    kp = proj_in.shape[0]
    kq = proj_out.shape[0]
    d = lax.axis_index("dp")
    f = lax.axis_index("fsdp")
    g = d * n_f + f
    z = f // PLANE
    y = (f // 2) % 2
    c = f % 2
    h = g // 2
    n_chip = n_all // 2

    def at(fi):
        return {"dp": d, "fsdp": fi}

    def device(gi):
        return {"dp": gi // n_f, "fsdp": gi % n_f}

    own = pltpu.make_async_copy(acts, xbuf.at[f], own_sem.at[0])
    own.start()
    ogc = pltpu.make_async_copy(out_grad, og, own_sem.at[1])
    ogc.start()
    weights = []
    for k in range(n_chunk):
        for s, w in enumerate((gate_w, up_w)):
            cp = pltpu.make_async_copy(
                w.at[pl.ds(128 * k, 128)], wbuf.at[k, pl.ds(128 * s, 128)], w_sem.at[2 * k + s]
            )
            cp.start()
            weights.append(cp)

    barrier = pltpu.get_barrier_semaphore()

    def greet(o, carry):
        pl.semaphore_signal(barrier, inc=1, device_id=device((g + o) % n_all), device_id_type=MESH)
        return carry

    lax.fori_loop(1, n_all, greet, 0)
    pl.semaphore_wait(barrier, n_all - 1)

    def push(block, target, send, recv):
        return pltpu.make_async_remote_copy(
            src_ref=xbuf.at[block], dst_ref=xbuf.at[block], send_sem=send, recv_sem=recv,
            device_id=at(target), device_id_type=MESH,
        )

    def z_up(p):
        return push(p * PLANE + y * 2 + c, f + PLANE, zu_s.at[p], zr_sem.at[p])

    def z_down(p):
        return push(p * PLANE + y * 2 + c, f - PLANE, zd_s.at[p], zr_sem.at[p])

    def y_send(p):
        return push(p * PLANE + y * 2 + c, z * PLANE + (1 - y) * 2 + c, ys_s.at[p], yr_sem.at[p])

    half = rows // 2

    def y_half(p):
        block = p * PLANE + y * 2 + c
        return pltpu.make_async_remote_copy(
            src_ref=xbuf.at[block, pl.ds(half, half)], dst_ref=xbuf.at[block, pl.ds(half, half)],
            send_sem=ys_s.at[p], recv_sem=yr_sem.at[p],
            device_id=at(z * PLANE + (1 - y) * 2 + c), device_id_type=MESH,
        )

    def w_send(p, step):
        block = p * PLANE + (1 - y) * 2 + c
        return pltpu.make_async_remote_copy(
            src_ref=xbuf.at[block, pl.ds(0, half)], dst_ref=xbuf.at[block, pl.ds(0, half)],
            send_sem=w_s.at[p], recv_sem=w_r.at[p],
            device_id=at(f + step * PLANE), device_id_type=MESH,
        )

    def by_y(p, fn):
        parted = (p != z) & ((p == 0) | (p == n_z - 1))
        pl.when(parted)(lambda: fn(y_half(p)))
        pl.when(jnp.logical_not(parted))(lambda: fn(y_send(p)))

    def by_w(p, fn):
        pl.when((p == 0) & (z < n_z - 1))(lambda: fn(w_send(p, 1)))
        pl.when((p == n_z - 1) & (z > 0))(lambda: fn(w_send(p, -1)))

    def c_send(p, yy):
        return push(p * PLANE + yy * 2 + c, z * PLANE + y * 2 + 1 - c, cs_s.at[2 * p + yy], cr_sem.at[2 * p + yy])

    def when(cond, fn):
        if cond is None:
            fn()
        else:
            pl.when(cond)(fn)

    def planes(r):
        if r == 0:
            return [(z, None, 0)]
        return [(z - r, z - r >= 0, 1), (z + r, z + r < n_z, -1)]

    def spread(r):
        for p, ok, way in planes(r):
            def go(p=p, way=way):
                if way != 0:
                    z_up(p).wait_recv()
                if way >= 0:
                    pl.when(z < n_z - 1)(lambda: z_up(p).start())
                if way <= 0:
                    pl.when(z > 0)(lambda: z_down(p).start())
                by_y(p, lambda cp: cp.start())
                c_send(p, y).start()
            when(ok, go)

    def part_copy(p, q):
        return pltpu.make_async_remote_copy(
            src_ref=part.at[p, pl.ds(16 * q, 16)], dst_ref=lrecv.at[f],
            send_sem=part_s.at[p * PLANE + q], recv_sem=part_r.at[f],
            device_id=at(p * PLANE + q), device_id_type=MESH,
        )

    def work(r):
        for p, ok, _ in planes(r):
            def relay(p=p):
                by_y(p, lambda cp: cp.wait_recv())
                pl.when((p != z) & ((p == 0) | (p == n_z - 1)))(lambda: w_send(p, 0).wait_recv())
                by_w(p, lambda cp: cp.start())
                c_send(p, 1 - y).start()
            when(ok, relay)
        for p, ok, _ in planes(r):
            def go(p=p):
                c_send(p, 0).wait_recv()
                c_send(p, 1).wait_recv()

                def chunk(k, total):
                    x = xbuf[pl.ds(p * PLANE, PLANE)].reshape(prow, acts.shape[1])
                    both = lax.dot_general(wbuf[k], x, NT, preferred_element_type=F32)
                    gate = both[:128]
                    hidden = (gate / (1.0 + jnp.exp(-gate)) * both[128:]).astype(BF16)
                    return total + lax.dot_general(pin[k], hidden, NN, preferred_element_type=F32)

                total = lax.fori_loop(0, n_chunk, chunk, jnp.zeros((kp, prow), F32))
                part[p] = total
                for q in range(PLANE):
                    mine = p * PLANE + q == f
                    pl.when(jnp.logical_not(mine))(lambda q=q: part_copy(p, q).start())

                    def keep(q=q):
                        lrecv[f] = part[p, pl.ds(16 * q, 16)]
                    pl.when(mine)(keep)
            when(ok, go)

    own.wait()
    spread(0)

    ogc.wait()
    for k in range(n_chunk):
        pin[k] = proj_in[:, pl.ds(128 * k, 128)]
    right = lax.dot_general(og[...], proj_out[...], NT, preferred_element_type=F32)
    rbuf[c, h] = jnp.concatenate([right[:rows // 2], right[rows // 2:]], axis=1)

    def share(buf, send, recv, o):
        return pltpu.make_async_remote_copy(
            src_ref=buf.at[c, h], dst_ref=buf.at[c, h], send_sem=send.at[o], recv_sem=recv.at[o],
            device_id=device(((h + o) % n_chip) * 2 + c), device_id_type=MESH,
        )

    def swap(buf, send, recv):
        return pltpu.make_async_remote_copy(
            src_ref=buf.at[c], dst_ref=buf.at[c], send_sem=send.at[0], recv_sem=recv.at[0],
            device_id=at(f + 1 - 2 * c), device_id_type=MESH,
        )

    def each(fn):
        def body(o, carry):
            fn(o)
            return carry
        lax.fori_loop(1, n_chip, body, 0)

    each(lambda o: share(rbuf, r_s, r_r, o).start())
    for cp in weights:
        cp.wait()

    for r in range(1, n_z):
        spread(r)
        work(r - 1)
        if r == 1:
            each(lambda o: share(rbuf, r_s, r_r, o).wait())
            swap(rbuf, r_s, r_r).start()

    swap(rbuf, r_s, r_r).wait()
    lane = lax.broadcasted_iota(jnp.int32, (kq, 2 * rows), 1)
    low = lane // (rows // 2) % 2 == 0
    for b in range(n_chip):
        one, two = rbuf[0, b], rbuf[1, b]
        tall = jnp.concatenate([one, one, two, two], axis=0).T
        vt[:, pl.ds(2 * rows * b, 2 * rows)] = jnp.where(low, tall[:kq], tall[kq:])
    work(n_z - 1)

    def wait_part(s, carry):
        def go():
            pltpu.make_async_remote_copy(
                src_ref=lrecv.at[s], dst_ref=lrecv.at[s], send_sem=part_s.at[s], recv_sem=part_r.at[s],
                device_id=at(f), device_id_type=MESH,
            ).wait_recv()
        pl.when(s != f)(go)
        return carry

    lax.fori_loop(0, n_f, wait_part, 0)
    total = lrecv[0]
    for s in range(1, n_f):
        total = total + lrecv[s]
    lbuf[c, h] = total.astype(BF16)
    each(lambda o: share(lbuf, l_s, l_r, o).start())
    each(lambda o: share(lbuf, l_s, l_r, o).wait())
    swap(lbuf, l_s, l_r).start()
    swap(lbuf, l_s, l_r).wait()

    for b in range(n_all):
        q = b % PLANE
        tok = (b // n_f) * n_z + (b % n_f) // PLANE
        ut[pl.ds(16 * q, 16), pl.ds(prow * tok, prow)] = lbuf[b % 2, b // 2].astype(F32)

    for r in range(n_z):
        for p, ok, way in planes(r):
            def fin(p=p, way=way):
                if way >= 0:
                    pl.when(z < n_z - 1)(lambda: z_up(p).wait_send())
                if way <= 0:
                    pl.when(z > 0)(lambda: z_down(p).wait_send())
                by_y(p, lambda cp: cp.wait_send())
                by_w(p, lambda cp: cp.wait_send())
                c_send(p, 0).wait_send()
                c_send(p, 1).wait_send()
                for q in range(PLANE):
                    pl.when(p * PLANE + q != f)(lambda q=q: part_copy(p, q).wait_send())
            when(ok, fin)


def moment_kernel(width, cols, group, ut, vt, feat, gram, a_rows, raw_s):
    k = pl.program_id(0)
    d = lax.axis_index("dp")
    f = lax.axis_index("fsdp")
    tokens = ut.shape[1]
    kq = vt.shape[0]

    def z_rows(first, count):
        v = vt[...]
        return jnp.concatenate([(ut[pl.ds(first + i, 1), :] * v).astype(BF16) for i in range(count)], axis=0)

    def head():
        a_rows[...] = z_rows(f * width, width)
        for e in range(group // LEN):
            span = pl.ds(pl.multiple_of(d * group + e * LEN, LEN), LEN)
            raw = lax.dot_general(ut[:, span], vt[:, span], NT, precision=lax.Precision.HIGHEST, preferred_element_type=F32)
            raw_s[...] = raw / jnp.sqrt(jnp.sum(raw * raw, keepdims=True) + 1e-06)
            for i in range(width):
                feat[pl.ds(e, 1), pl.ds(kq * i, kq)] = raw_s[pl.ds(f * width + i, 1), :]

    pl.when(k == 0)(head)
    block = lax.dot_general(a_rows[...], z_rows(d * cols + 4 * k, 4), NT, preferred_element_type=F32)
    gram[...] = block * (1.0 / tokens)


def fused(n_f, n_dp, acts, out_grad, gate_weight, up_weight, proj_in, proj_out):
    rows, depth = acts.shape
    units = gate_weight.shape[0]
    kp, kq = proj_in.shape[1], proj_out.shape[1]
    n_all = n_f * n_dp
    tokens = rows * n_all
    n_chunk = units // 128
    n_z = n_f // PLANE
    width = kp // n_f
    examples = rows * n_f // LEN
    dma = pltpu.SemaphoreType.DMA
    hbm = pl.BlockSpec(memory_space=pl.ANY)
    vmem = pl.BlockSpec(memory_space=pltpu.VMEM)
    ut, vt = pl.pallas_call(
        functools.partial(fused_kernel, n_f, n_dp),
        out_shape=(
            jax.ShapeDtypeStruct((kp, tokens), F32),
            jax.ShapeDtypeStruct((kq, tokens), F32),
        ),
        in_specs=[hbm, hbm, hbm, hbm, vmem, vmem],
        out_specs=(vmem, vmem),
        scratch_shapes=[
            pltpu.VMEM((n_f, rows, depth), BF16),
            pltpu.VMEM((n_chunk, 256, depth), BF16),
            pltpu.VMEM((n_chunk, kp, 128), BF16),
            pltpu.VMEM((rows, depth), BF16),
            pltpu.VMEM((n_z, kp, rows * PLANE), F32),
            pltpu.VMEM((n_f, 16, rows * PLANE), F32),
            pltpu.VMEM((2, n_all // 2, rows // 2, 2 * kq), F32),
            pltpu.VMEM((2, n_all // 2, 16, rows * PLANE), BF16),
            dma((2,)), dma((2 * n_chunk,)), dma((n_z,)), dma((n_z,)), dma((2 * n_z,)),
            dma((n_z,)), dma((n_z,)), dma((n_z,)), dma((2 * n_z,)), dma((n_z,)), dma((n_z,)),
            dma((n_f,)), dma((n_f,)), dma((n_all // 2,)), dma((n_all // 2,)), dma((n_all // 2,)), dma((n_all // 2,)),
        ],
        compiler_params=pltpu.CompilerParams(
            collective_id=0, has_side_effects=True, vmem_limit_bytes=56 * 1024 * 1024
        ),
    )(acts, out_grad, gate_weight, up_weight, proj_in.T, proj_out.T)
    cols = kp // n_dp
    whole = lambda k: (0, 0)
    return pl.pallas_call(
        functools.partial(moment_kernel, width, cols, tokens // n_dp),
        grid=(cols // 4,),
        out_shape=(
            jax.ShapeDtypeStruct((examples, width * kq), F32),
            jax.ShapeDtypeStruct((width * kq, cols * kq), F32),
        ),
        in_specs=[pl.BlockSpec((kp, tokens), whole), pl.BlockSpec((kq, tokens), whole)],
        out_specs=(
            pl.BlockSpec((examples, width * kq), whole),
            pl.BlockSpec((width * kq, 4 * kq), lambda k: (0, k)),
        ),
        scratch_shapes=[pltpu.VMEM((width * kq, tokens), BF16), pltpu.VMEM((kp, kq), F32)],
        compiler_params=pltpu.CompilerParams(vmem_limit_bytes=24 * 1024 * 1024),
    )(ut, vt)


def solution(mesh):
    n_f, n_dp = mesh.shape["fsdp"], mesh.shape["dp"]

    def run(acts, out_grad, gate_weight, up_weight, proj_in, proj_out):
        rows, units = acts.shape[0], gate_weight.shape[0]
        fits = (
            n_f % PLANE == 0
            and (PLANE * rows) % 128 == 0
            and rows % 32 == 0
            and units % 128 == 0
            and proj_out.shape[1] == 64
            and (2 * rows) % 128 == 0
            and proj_in.shape[1] == 16 * PLANE
            and proj_in.shape[1] % n_f == 0
            and proj_in.shape[1] % (4 * n_dp) == 0
            and (rows * n_f) % LEN == 0
        )
        if fits:
            return fused(n_f, n_dp, acts, out_grad, gate_weight, up_weight, proj_in, proj_out)
        return local(acts, out_grad, gate_weight, up_weight, proj_in, proj_out)

    in_specs = (
        P(("dp", "fsdp"), None),
        P(("dp", "fsdp"), None),
        P("fsdp", None),
        P("fsdp", None),
        P("fsdp", None),
        P(),
    )
    out_specs = (P("dp", "fsdp"), P("fsdp", "dp"))
    return jax.shard_map(run, mesh=mesh, in_specs=in_specs, out_specs=out_specs, check_vma=False)
```

```python
import functools

import jax
import jax.numpy as jnp
from jax import lax
from jax.experimental import pallas as pl
from jax.experimental.pallas import tpu as pltpu
from jax.sharding import PartitionSpec as P

LEN = 512


def outer_rows(u_part, v_rows):
    return (u_part[:, :, None] * v_rows[:, None, :]).reshape(
        u_part.shape[0], u_part.shape[1] * v_rows.shape[1]
    )


def moment_rows(u_part, u_cols, v_rows):
    a_rows = outer_rows(u_part, v_rows)
    z_cols = outer_rows(u_cols, v_rows)
    return lax.dot_general(
        a_rows,
        z_cols,
        (((0,), (0,)), ((), ())),
        precision=lax.Precision.HIGHEST,
        preferred_element_type=jnp.float32,
    )


def local(acts, out_grad, gate_weight, up_weight, proj_in, proj_out):
    n_fsdp = lax.axis_size("fsdp")
    n_dp = lax.axis_size("dp")
    contract = (((1,), (1,)), ((), ()))
    piece = lax.all_gather(acts, "fsdp", axis=0, tiled=True)
    gate = lax.dot_general(piece, gate_weight, contract, preferred_element_type=jnp.float32)
    upper = lax.dot_general(piece, up_weight, contract, preferred_element_type=jnp.float32)
    hidden = (jax.nn.silu(gate) * upper).astype(jnp.bfloat16)
    part_in = jnp.dot(hidden, proj_in, preferred_element_type=jnp.float32)
    left = lax.psum(part_in, "fsdp")
    part_out = jnp.dot(out_grad, proj_out, preferred_element_type=jnp.float32)
    right = lax.all_gather(part_out, "fsdp", axis=0, tiled=True)
    rows = left.shape[0]
    total_tokens = rows * n_dp
    kp_size = left.shape[1]
    kq_size = right.shape[1]
    row_width = kp_size // n_fsdp
    first = lax.axis_index("fsdp") * row_width
    mine = lax.dynamic_slice_in_dim(left, first, row_width, 1)
    examples = rows // LEN
    left_ex = left.reshape(examples, LEN, kp_size)
    right_ex = right.reshape(examples, LEN, kq_size)
    mine_ex = mine.reshape(examples, LEN, row_width)
    raw = jnp.einsum("elw,elq->ewq", mine_ex, right_ex, precision=lax.Precision.HIGHEST).reshape(
        examples, row_width * kq_size
    )
    squared = lax.psum(jnp.sum(raw * raw, axis=1), "fsdp")
    features = raw / jnp.sqrt(squared + 1e-06)[:, None]

    def add_example(index, total):
        u_rows = lax.dynamic_index_in_dim(left_ex, index, 0, keepdims=False)
        v_rows = lax.dynamic_index_in_dim(right_ex, index, 0, keepdims=False)
        u_part = lax.dynamic_index_in_dim(mine_ex, index, 0, keepdims=False)
        return total + moment_rows(u_part, u_rows, v_rows)

    start_total = jnp.zeros((row_width * kq_size, kp_size * kq_size), jnp.float32)
    partial_value = lax.fori_loop(0, examples, add_example, start_total)
    gram = lax.psum_scatter(
        partial_value / jnp.float32(total_tokens), "dp", scatter_dimension=1, tiled=True
    )
    return (features, gram)


MESH = pl.DeviceIdType.MESH
NT = (((1,), (1,)), ((), ()))
NN = (((1,), (0,)), ((), ()))
F32 = jnp.float32
BF16 = jnp.bfloat16
PLANE = 4


def fused_kernel(n_f, n_dp, acts, out_grad, gate_w, up_w, proj_in, proj_out, ut, vt,
                 xbuf, wbuf, pin, og, part, lrecv, rbuf, lbuf,
                 own_sem, w_sem, zr_sem, yr_sem, cr_sem, zu_s, zd_s, ys_s, cs_s, w_s, w_r,
                 part_s, part_r, r_s, r_r, l_s, l_r):
    n_z = n_f // PLANE
    n_all = n_f * n_dp
    rows = acts.shape[0]
    units = gate_w.shape[0]
    n_chunk = units // 128
    prow = rows * PLANE
    kp = proj_in.shape[0]
    kq = proj_out.shape[0]
    d = lax.axis_index("dp")
    f = lax.axis_index("fsdp")
    g = d * n_f + f
    z = f // PLANE
    y = (f // 2) % 2
    c = f % 2
    h = g // 2
    n_chip = n_all // 2

    def at(fi):
        return {"dp": d, "fsdp": fi}

    def device(gi):
        return {"dp": gi // n_f, "fsdp": gi % n_f}

    barrier = pltpu.get_barrier_semaphore()

    def greet(o, carry):
        pl.semaphore_signal(barrier, inc=1, device_id=device((g + o) % n_all), device_id_type=MESH)
        return carry

    lax.fori_loop(1, n_all, greet, 0)
    own = pltpu.make_async_copy(acts, xbuf.at[f], own_sem.at[0])
    own.start()
    ogc = pltpu.make_async_copy(out_grad, og, own_sem.at[1])
    ogc.start()
    weights = []
    for k in range(n_chunk):
        for s, w in enumerate((gate_w, up_w)):
            cp = pltpu.make_async_copy(
                w.at[pl.ds(128 * k, 128)], wbuf.at[k, pl.ds(128 * s, 128)], w_sem.at[2 * k + s]
            )
            cp.start()
            weights.append(cp)

    pl.semaphore_wait(barrier, n_all - 1)

    def push(block, target, send, recv):
        return pltpu.make_async_remote_copy(
            src_ref=xbuf.at[block], dst_ref=xbuf.at[block], send_sem=send, recv_sem=recv,
            device_id=at(target), device_id_type=MESH,
        )

    def z_up(p):
        return push(p * PLANE + y * 2 + c, f + PLANE, zu_s.at[p], zr_sem.at[p])

    def z_down(p):
        return push(p * PLANE + y * 2 + c, f - PLANE, zd_s.at[p], zr_sem.at[p])

    def y_send(p):
        return push(p * PLANE + y * 2 + c, z * PLANE + (1 - y) * 2 + c, ys_s.at[p], yr_sem.at[p])

    half = rows // 2

    def y_half(p):
        block = p * PLANE + y * 2 + c
        return pltpu.make_async_remote_copy(
            src_ref=xbuf.at[block, pl.ds(half, half)], dst_ref=xbuf.at[block, pl.ds(half, half)],
            send_sem=ys_s.at[p], recv_sem=yr_sem.at[p],
            device_id=at(z * PLANE + (1 - y) * 2 + c), device_id_type=MESH,
        )

    def w_send(p, step):
        block = p * PLANE + (1 - y) * 2 + c
        return pltpu.make_async_remote_copy(
            src_ref=xbuf.at[block, pl.ds(0, half)], dst_ref=xbuf.at[block, pl.ds(0, half)],
            send_sem=w_s.at[p], recv_sem=w_r.at[p],
            device_id=at(f + step * PLANE), device_id_type=MESH,
        )

    def by_y(p, fn):
        parted = (p != z) & ((p == 0) | (p == n_z - 1))
        pl.when(parted)(lambda: fn(y_half(p)))
        pl.when(jnp.logical_not(parted))(lambda: fn(y_send(p)))

    def by_w(p, fn):
        pl.when((p == 0) & (z < n_z - 1))(lambda: fn(w_send(p, 1)))
        pl.when((p == n_z - 1) & (z > 0))(lambda: fn(w_send(p, -1)))

    def c_send(p, yy):
        return push(p * PLANE + yy * 2 + c, z * PLANE + y * 2 + 1 - c, cs_s.at[2 * p + yy], cr_sem.at[2 * p + yy])

    def when(cond, fn):
        if cond is None:
            fn()
        else:
            pl.when(cond)(fn)

    def planes(r):
        if r == 0:
            return [(z, None, 0)]
        return [(z - r, z - r >= 0, 1), (z + r, z + r < n_z, -1)]

    def spread(r):
        for p, ok, way in planes(r):
            def go(p=p, way=way):
                if way != 0:
                    z_up(p).wait_recv()
                if way >= 0:
                    pl.when(z < n_z - 1)(lambda: z_up(p).start())
                if way <= 0:
                    pl.when(z > 0)(lambda: z_down(p).start())
                by_y(p, lambda cp: cp.start())
                c_send(p, y).start()
            when(ok, go)

    def part_copy(p, q):
        return pltpu.make_async_remote_copy(
            src_ref=part.at[p, pl.ds(16 * q, 16)], dst_ref=lrecv.at[f],
            send_sem=part_s.at[p * PLANE + q], recv_sem=part_r.at[f],
            device_id=at(p * PLANE + q), device_id_type=MESH,
        )

    def work(r):
        for p, ok, _ in planes(r):
            def relay(p=p):
                by_y(p, lambda cp: cp.wait_recv())
                pl.when((p != z) & ((p == 0) | (p == n_z - 1)))(lambda: w_send(p, 0).wait_recv())
                by_w(p, lambda cp: cp.start())
                c_send(p, 1 - y).start()
            when(ok, relay)
        for p, ok, _ in planes(r):
            def go(p=p):
                c_send(p, 0).wait_recv()
                c_send(p, 1).wait_recv()

                def chunk(k, total):
                    x = xbuf[pl.ds(p * PLANE, PLANE)].reshape(prow, acts.shape[1])
                    both = lax.dot_general(wbuf[k], x, NT, preferred_element_type=F32)
                    gate = both[:128]
                    hidden = (gate / (1.0 + jnp.exp(-gate)) * both[128:]).astype(BF16)
                    return total + lax.dot_general(pin[k], hidden, NN, preferred_element_type=F32)

                total = lax.fori_loop(0, n_chunk, chunk, jnp.zeros((kp, prow), F32))
                part[p] = total
                for q in range(PLANE):
                    mine = p * PLANE + q == f
                    pl.when(jnp.logical_not(mine))(lambda q=q: part_copy(p, q).start())

                    def keep(q=q):
                        lrecv[f] = part[p, pl.ds(16 * q, 16)]
                    pl.when(mine)(keep)
            when(ok, go)

    own.wait()
    spread(0)

    ogc.wait()
    for k in range(n_chunk):
        pin[k] = proj_in[:, pl.ds(128 * k, 128)]
    right = lax.dot_general(og[...], proj_out[...], NT, preferred_element_type=F32)
    rbuf[c, h] = jnp.concatenate([right[:rows // 2], right[rows // 2:]], axis=1)

    def share(buf, send, recv, o):
        return pltpu.make_async_remote_copy(
            src_ref=buf.at[c, h], dst_ref=buf.at[c, h], send_sem=send.at[o], recv_sem=recv.at[o],
            device_id=device(((h + o) % n_chip) * 2 + c), device_id_type=MESH,
        )

    def swap(buf, send, recv):
        return pltpu.make_async_remote_copy(
            src_ref=buf.at[c], dst_ref=buf.at[c], send_sem=send.at[0], recv_sem=recv.at[0],
            device_id=at(f + 1 - 2 * c), device_id_type=MESH,
        )

    def each(fn):
        def body(o, carry):
            fn(o)
            return carry
        lax.fori_loop(1, n_chip, body, 0)

    each(lambda o: share(rbuf, r_s, r_r, o).start())
    for cp in weights:
        cp.wait()

    for r in range(1, n_z):
        spread(r)
        work(r - 1)
        if r == 1:
            each(lambda o: share(rbuf, r_s, r_r, o).wait())
            swap(rbuf, r_s, r_r).start()

    swap(rbuf, r_s, r_r).wait()
    lane = lax.broadcasted_iota(jnp.int32, (kq, 2 * rows), 1)
    low = lane // (rows // 2) % 2 == 0
    for b in range(n_chip):
        one, two = rbuf[0, b], rbuf[1, b]
        tall = jnp.concatenate([one, one, two, two], axis=0).T
        vt[:, pl.ds(2 * rows * b, 2 * rows)] = jnp.where(low, tall[:kq], tall[kq:])
    work(n_z - 1)

    def wait_part(s, carry):
        def go():
            pltpu.make_async_remote_copy(
                src_ref=lrecv.at[s], dst_ref=lrecv.at[s], send_sem=part_s.at[s], recv_sem=part_r.at[s],
                device_id=at(f), device_id_type=MESH,
            ).wait_recv()
        pl.when(s != f)(go)
        return carry

    lax.fori_loop(0, n_f, wait_part, 0)
    total = lrecv[0]
    for s in range(1, n_f):
        total = total + lrecv[s]
    lbuf[c, h] = total.astype(BF16)
    each(lambda o: share(lbuf, l_s, l_r, o).start())
    each(lambda o: share(lbuf, l_s, l_r, o).wait())
    swap(lbuf, l_s, l_r).start()
    swap(lbuf, l_s, l_r).wait()

    for b in range(n_all):
        q = b % PLANE
        tok = (b // n_f) * n_z + (b % n_f) // PLANE
        ut[pl.ds(16 * q, 16), pl.ds(prow * tok, prow)] = lbuf[b % 2, b // 2].astype(F32)

    for r in range(n_z):
        for p, ok, way in planes(r):
            def fin(p=p, way=way):
                if way >= 0:
                    pl.when(z < n_z - 1)(lambda: z_up(p).wait_send())
                if way <= 0:
                    pl.when(z > 0)(lambda: z_down(p).wait_send())
                by_y(p, lambda cp: cp.wait_send())
                by_w(p, lambda cp: cp.wait_send())
                c_send(p, 0).wait_send()
                c_send(p, 1).wait_send()
                for q in range(PLANE):
                    pl.when(p * PLANE + q != f)(lambda q=q: part_copy(p, q).wait_send())
            when(ok, fin)


def moment_kernel(width, cols, group, ut, vt, feat, gram, a_rows, raw_s):
    k = pl.program_id(0)
    d = lax.axis_index("dp")
    f = lax.axis_index("fsdp")
    tokens = ut.shape[1]
    kq = vt.shape[0]

    def z_rows(first, count):
        v = vt[...]
        return jnp.concatenate([(ut[pl.ds(first + i, 1), :] * v).astype(BF16) for i in range(count)], axis=0)

    def head():
        a_rows[...] = z_rows(f * width, width)
        for e in range(group // LEN):
            span = pl.ds(pl.multiple_of(d * group + e * LEN, LEN), LEN)
            raw = lax.dot_general(ut[:, span], vt[:, span], NT, precision=lax.Precision.HIGHEST, preferred_element_type=F32)
            raw_s[...] = raw / jnp.sqrt(jnp.sum(raw * raw, keepdims=True) + 1e-06)
            for i in range(width):
                feat[pl.ds(e, 1), pl.ds(kq * i, kq)] = raw_s[pl.ds(f * width + i, 1), :]

    pl.when(k == 0)(head)
    block = lax.dot_general(a_rows[...], z_rows(d * cols + 4 * k, 4), NT, preferred_element_type=F32)
    gram[...] = block * (1.0 / tokens)


def fused(n_f, n_dp, acts, out_grad, gate_weight, up_weight, proj_in, proj_out):
    rows, depth = acts.shape
    units = gate_weight.shape[0]
    kp, kq = proj_in.shape[1], proj_out.shape[1]
    n_all = n_f * n_dp
    tokens = rows * n_all
    n_chunk = units // 128
    n_z = n_f // PLANE
    width = kp // n_f
    examples = rows * n_f // LEN
    dma = pltpu.SemaphoreType.DMA
    hbm = pl.BlockSpec(memory_space=pl.ANY)
    vmem = pl.BlockSpec(memory_space=pltpu.VMEM)
    ut, vt = pl.pallas_call(
        functools.partial(fused_kernel, n_f, n_dp),
        out_shape=(
            jax.ShapeDtypeStruct((kp, tokens), F32),
            jax.ShapeDtypeStruct((kq, tokens), F32),
        ),
        in_specs=[hbm, hbm, hbm, hbm, vmem, vmem],
        out_specs=(vmem, vmem),
        scratch_shapes=[
            pltpu.VMEM((n_f, rows, depth), BF16),
            pltpu.VMEM((n_chunk, 256, depth), BF16),
            pltpu.VMEM((n_chunk, kp, 128), BF16),
            pltpu.VMEM((rows, depth), BF16),
            pltpu.VMEM((n_z, kp, rows * PLANE), F32),
            pltpu.VMEM((n_f, 16, rows * PLANE), F32),
            pltpu.VMEM((2, n_all // 2, rows // 2, 2 * kq), F32),
            pltpu.VMEM((2, n_all // 2, 16, rows * PLANE), BF16),
            dma((2,)), dma((2 * n_chunk,)), dma((n_z,)), dma((n_z,)), dma((2 * n_z,)),
            dma((n_z,)), dma((n_z,)), dma((n_z,)), dma((2 * n_z,)), dma((n_z,)), dma((n_z,)),
            dma((n_f,)), dma((n_f,)), dma((n_all // 2,)), dma((n_all // 2,)), dma((n_all // 2,)), dma((n_all // 2,)),
        ],
        compiler_params=pltpu.CompilerParams(
            collective_id=0, has_side_effects=True, vmem_limit_bytes=56 * 1024 * 1024
        ),
    )(acts, out_grad, gate_weight, up_weight, proj_in.T, proj_out.T)
    cols = kp // n_dp
    whole = lambda k: (0, 0)
    return pl.pallas_call(
        functools.partial(moment_kernel, width, cols, tokens // n_dp),
        grid=(cols // 4,),
        out_shape=(
            jax.ShapeDtypeStruct((examples, width * kq), F32),
            jax.ShapeDtypeStruct((width * kq, cols * kq), F32),
        ),
        in_specs=[pl.BlockSpec((kp, tokens), whole), pl.BlockSpec((kq, tokens), whole)],
        out_specs=(
            pl.BlockSpec((examples, width * kq), whole),
            pl.BlockSpec((width * kq, 4 * kq), lambda k: (0, k)),
        ),
        scratch_shapes=[pltpu.VMEM((width * kq, tokens), BF16), pltpu.VMEM((kp, kq), F32)],
        compiler_params=pltpu.CompilerParams(vmem_limit_bytes=24 * 1024 * 1024),
    )(ut, vt)


def solution(mesh):
    n_f, n_dp = mesh.shape["fsdp"], mesh.shape["dp"]

    def run(acts, out_grad, gate_weight, up_weight, proj_in, proj_out):
        rows, units = acts.shape[0], gate_weight.shape[0]
        fits = (
            n_f % PLANE == 0
            and (PLANE * rows) % 128 == 0
            and rows % 32 == 0
            and units % 128 == 0
            and proj_out.shape[1] == 64
            and (2 * rows) % 128 == 0
            and proj_in.shape[1] == 16 * PLANE
            and proj_in.shape[1] % n_f == 0
            and proj_in.shape[1] % (4 * n_dp) == 0
            and (rows * n_f) % LEN == 0
        )
        if fits:
            return fused(n_f, n_dp, acts, out_grad, gate_weight, up_weight, proj_in, proj_out)
        return local(acts, out_grad, gate_weight, up_weight, proj_in, proj_out)

    in_specs = (
        P(("dp", "fsdp"), None),
        P(("dp", "fsdp"), None),
        P("fsdp", None),
        P("fsdp", None),
        P("fsdp", None),
        P(),
    )
    out_specs = (P("dp", "fsdp"), P("fsdp", "dp"))
    return jax.shard_map(run, mesh=mesh, in_specs=in_specs, out_specs=out_specs, check_vma=False)
```
